512 devices in a mesh: section: 16 (over y, core), ctx: 8 (over z), tp: 4 (over x).
Axes of the slice: x: 4, y: 8, z: 8, core: 2. Of those that a mesh axis runs over, the one named last changes fastest.
Arguments:
- query_rows: bfloat16 [16, 1024, 16384], P('section', 'ctx', 'tp'), may hold values from -56 to 56
- key_rows: bfloat16 [16, 1024, 1024], P('section', 'ctx', 'tp'), may hold values from -16 to 16
- value_rows: bfloat16 [16, 1024, 1024], P('section', 'ctx', 'tp'), may hold values from -6 to 6
- positions: int32 [16, 1024], P('section'), may hold values from 0 to 131071, as said below
Outputs:
- attended: bfloat16 [16, 1024, 16384], P('section', 'ctx', 'tp')
The draws below stay inside these ranges and needn't reach their ends.
Inputs may be any that keep to these rules, and one draw needn't show every extreme that they name: For each section, the 1024 positions are the run start, start + 1, ..., start + 1023 laid out in blocks of 64 consecutive ascending positions whose order along the sequence dimension is a permutation of the 16 blocks; start is 0 for section 0 and 130048 for section 15.
All inputs are finite; a program needn't handle non-finite values.
Results may differ from the reference program's by a relative error of at most 0.0084.
Values may be sent and summed in bfloat16 or wider, within the bound.
No kernel may reach another device: no remote copies, remote signals or barrier semaphores. Data moves between devices by JAX's collectives and lax.ppermute only.
A program may use at most 64 MiB of HBM per device.

```python
import math
import jax
import jax.numpy as jnp
import numpy as np
from jax import lax

HEADS = 128
KV_HEADS = 8
HEAD_DIM = 128
SECTIONS = 16
SEQ = 1024
BLK = 64


def draw_query_rows(key, part):
    key = jax.random.fold_in(key, 11)
    base_draw = jnp.clip(jax.random.normal(key, (SECTIONS, SEQ, HEADS, HEAD_DIM), jnp.float32), -6.0, 6.0)
    return base_draw.reshape(SECTIONS, SEQ, HEADS * HEAD_DIM).astype(jnp.bfloat16)


def draw_key_rows(key, part):
    key = jax.random.fold_in(key, 12)
    key_normal = jax.random.fold_in(key, 0)
    base_draw = jnp.clip(jax.random.normal(key_normal, (SECTIONS, SEQ, KV_HEADS, HEAD_DIM), jnp.float32), -4.0, 4.0)
    return base_draw.reshape(SECTIONS, SEQ, KV_HEADS * HEAD_DIM).astype(jnp.bfloat16)


def draw_positions(key, part):
    key = jax.random.fold_in(key, 13)
    key_perm, key_start = jax.random.split(key)
    block_count = SEQ // BLK
    orders = jax.vmap(lambda sub_key: jax.random.permutation(sub_key, block_count))(jax.random.split(key_perm, SECTIONS))
    start_limit = 131072 - SEQ
    starts = jax.random.randint(key_start, (SECTIONS,), 0, start_limit + 1)
    section_ids = jnp.arange(SECTIONS)
    starts = jnp.where(section_ids == 0, 0, jnp.where(section_ids == SECTIONS - 1, start_limit, starts))
    inner_ids = jnp.arange(BLK)
    placed = starts[:, None, None] + orders[:, :, None] * BLK + inner_ids[None, None, :]
    return placed.reshape(SECTIONS, SEQ).astype(jnp.int32)


def steps_of(own_key, shape, cuts, smallest, top_value):
    gain = 1.0
    for position, blocks in cuts:
        draws = jax.random.uniform(jax.random.fold_in(jax.random.fold_in(own_key, 6), position), (blocks,), jnp.float32, smallest / len(cuts), top_value / len(cuts))
        gain = gain * jnp.repeat(jnp.exp(draws), shape[position] // blocks).reshape((-1,) + (1,) * (len(shape) - 1 - position))
    return gain


def bell_draw(key, extent, deviation, bound, pieces=(), dtype=jnp.bfloat16):
    entries = deviation * jax.random.normal(key, extent, jnp.float32)
    if pieces:
        entries = entries * steps_of(key, extent, pieces, -0.22, 0.18)
    return jnp.clip(entries, -bound, bound).astype(dtype)


def setup_inputs(seed: int = 0) -> dict:
    seeds = jax.random.split(jax.random.key(seed), 5)
    return {
        "query_rows": draw_query_rows(jax.random.fold_in(seeds[4], 71), 0),
        "key_rows": draw_key_rows(jax.random.fold_in(seeds[4], 71), 0),
        "value_rows": bell_draw(seeds[2], (SECTIONS, SEQ, KV_HEADS * HEAD_DIM), 1.0, 6.0, ((0, 16), (1, 8), (2, 4))),
        "positions": draw_positions(jax.random.fold_in(seeds[4], 71), 0),
    }


def rope_tables(head_size):
    index_ids = np.arange(head_size // 2) * 1.0
    natural = 500000.0 ** (-2.0 * index_ids / head_size)
    wavelength = 2.0 * math.pi / natural
    smooth = (8192.0 / wavelength - 1.0) / 3.0
    blended = (1.0 - smooth) * natural / 8.0 + smooth * natural
    scaled = np.where(wavelength < 2048.0, natural, np.where(wavelength > 8192.0, natural / 8.0, blended))
    coarse = np.mod(1024.0 * scaled, 2.0 * math.pi)
    return (jnp.asarray(scaled, jnp.float32), jnp.asarray(coarse, jnp.float32))

def rotate(row_data, token_pos, head_count):
    count_rows = row_data.shape[0]
    head_size = row_data.shape[1] // head_count
    fine_freq, coarse = rope_tables(head_size)
    upper_part = (token_pos // 1024).astype(jnp.float32)
    lower_part = (token_pos % 1024).astype(jnp.float32)
    angles = upper_part[:, None] * coarse[None, :] + lower_part[:, None] * fine_freq[None, :]
    cosine = jnp.cos(angles)[:, None, :]
    sine_part = jnp.sin(angles)[:, None, :]
    heads_data = row_data.reshape(count_rows, head_count, head_size).astype(jnp.float32)
    front_half = heads_data[..., :head_size // 2]
    back_half = heads_data[..., head_size // 2:]
    turned = jnp.concatenate([front_half * cosine - back_half * sine_part, back_half * cosine + front_half * sine_part], axis=-1)
    return turned.reshape(count_rows, head_count * head_size).astype(jnp.bfloat16)

def one_group(queries, key_block, value_block, token_pos):
    scores = jnp.einsum('tgd,sd->gts', queries.astype(jnp.float32), key_block.astype(jnp.float32)) / math.sqrt(HEAD_DIM)
    allowed = token_pos[None, :] <= token_pos[:, None]
    masked = jnp.where(allowed[None], scores, -1e+30)
    row_max = lax.optimization_barrier(jnp.max(masked, axis=-1, keepdims=True))
    exponent = jnp.where(allowed[None], jnp.exp(masked - row_max), 0.0)
    denominator = lax.optimization_barrier(jnp.sum(exponent, axis=-1))
    weights = exponent.astype(jnp.bfloat16)
    numerator = jnp.einsum('gts,sd->gtd', weights.astype(jnp.float32), value_block.astype(jnp.float32))
    return (numerator / denominator[..., None]).astype(jnp.bfloat16)

def one_section(inputs):
    query_in, key_in, value_in, token_pos = inputs
    groups = HEADS // KV_HEADS
    rotated_queries = rotate(query_in, token_pos, HEADS).reshape(SEQ, KV_HEADS, groups, HEAD_DIM)
    rotated_keys = rotate(key_in, token_pos, KV_HEADS).reshape(SEQ, KV_HEADS, HEAD_DIM)
    value_heads = value_in.reshape(SEQ, KV_HEADS, HEAD_DIM)
    per_group = lax.map(lambda items: one_group(items[0], items[1], items[2], token_pos), (jnp.transpose(rotated_queries, (1, 0, 2, 3)), jnp.transpose(rotated_keys, (1, 0, 2)), jnp.transpose(value_heads, (1, 0, 2))))
    return jnp.transpose(per_group, (2, 0, 1, 3)).reshape(SEQ, HEADS * HEAD_DIM)

def reference(query_rows, key_rows, value_rows, positions):
    arrived = (jnp.roll(query_rows, 1, axis=0), jnp.roll(key_rows, 1, axis=0), jnp.roll(value_rows, 1, axis=0), positions)
    return lax.map(one_section, arrived)
```

```python
from functools import partial
import math

import jax
import jax.numpy as jnp
import numpy as np
from jax import lax
from jax.experimental import pallas as pl
from jax.experimental.pallas import tpu as pltpu
from jax.sharding import PartitionSpec as P

HEAD_DIM = 128
MASKED = -1e30
SCALE = math.log2(math.e) / math.sqrt(HEAD_DIM)
HEADS_PER_PASS = 2


def shifted(block, axis, distance):
    devices = range(lax.axis_size(axis))
    route = [((i - distance) % len(devices), i) for i in devices]
    return lax.ppermute(block, axis, route)


def rope_tables(head_size):
    index_ids = np.arange(head_size // 2) * 1.0
    natural = 500000.0 ** (-2.0 * index_ids / head_size)
    wavelength = 2.0 * math.pi / natural
    smooth = (8192.0 / wavelength - 1.0) / 3.0
    blended = (1.0 - smooth) * natural / 8.0 + smooth * natural
    scaled = np.where(
        wavelength < 2048.0, natural, np.where(wavelength > 8192.0, natural / 8.0, blended)
    )
    coarse = np.mod(1024.0 * scaled, 2.0 * math.pi)
    return (jnp.asarray(scaled, jnp.float32), jnp.asarray(coarse, jnp.float32))


def turn_tables(token_pos):
    fine_freq, coarse = rope_tables(HEAD_DIM)
    upper_part = (token_pos // 1024).astype(jnp.float32)
    lower_part = (token_pos % 1024).astype(jnp.float32)
    angles = upper_part[:, None] * coarse[None, :] + lower_part[:, None] * fine_freq[None, :]
    cosine, sine = jnp.cos(angles), jnp.sin(angles)
    return (
        jnp.concatenate([cosine, cosine], axis=-1),
        jnp.concatenate([-sine, sine], axis=-1),
    )


def turned(head, cosine, sine):
    head = head.astype(jnp.float32)
    return (head * cosine + pltpu.roll(head, HEAD_DIM // 2, 1) * sine).astype(jnp.bfloat16)


def spread_kernel(key_ref, value_ref, cosine_ref, sine_ref, *outs):
    cosine, sine = cosine_ref[...], sine_ref[...]
    for head, out in enumerate(outs):
        columns = pl.ds(head * HEAD_DIM, HEAD_DIM)
        keys = turned(key_ref[:, columns], cosine, sine)
        values = value_ref[:, columns]
        for owner in range(out.shape[0]):
            out[owner, :, :HEAD_DIM] = keys
            out[owner, :, HEAD_DIM:] = values


def spread(key_in, value_in, cosine, sine, owners):
    rows = key_in.shape[0]
    key_heads = key_in.shape[1] // HEAD_DIM
    shape = jax.ShapeDtypeStruct((owners, rows, 2 * HEAD_DIM), jnp.bfloat16)
    return pl.pallas_call(
        spread_kernel,
        out_shape=[shape] * key_heads,
        name="spread",
    )(key_in, value_in, cosine, sine)


def turn_kernel(query_ref, cosine_ref, sine_ref, out_ref):
    cosine, sine = cosine_ref[...], sine_ref[...]
    rows = query_ref.shape[0]
    for head in range(query_ref.shape[1] // HEAD_DIM):
        out_ref[head * rows : (head + 1) * rows, :] = turned(
            query_ref[:, head * HEAD_DIM : (head + 1) * HEAD_DIM], cosine, sine
        )


def turn_queries(query_in, cosine, sine):
    rows, width = query_in.shape
    heads = width // HEAD_DIM
    steps = 4
    return pl.pallas_call(
        turn_kernel,
        grid=(steps,),
        in_specs=[
            pl.BlockSpec((rows, width // steps), lambda i: (0, i)),
            pl.BlockSpec((rows, HEAD_DIM), lambda i: (0, 0)),
            pl.BlockSpec((rows, HEAD_DIM), lambda i: (0, 0)),
        ],
        out_specs=pl.BlockSpec((heads // steps * rows, HEAD_DIM), lambda i: (i, 0)),
        out_shape=jax.ShapeDtypeStruct((heads * rows, HEAD_DIM), jnp.bfloat16),
        name="turn",
    )(query_in, cosine, sine)


def attend_kernel(query_ref, gathered_ref, mask_ref, *rest):
    out_ref = rest[-1]
    rows = mask_ref.shape[1]
    tokens = mask_ref.shape[0]
    gathered = gathered_ref[...].reshape(tokens, 2 * HEAD_DIM)
    keys = jnp.concatenate([gathered[:, :HEAD_DIM], mask_ref[...]], axis=1)
    values = jnp.concatenate(
        [gathered[:, HEAD_DIM:], jnp.ones((tokens, HEAD_DIM), jnp.bfloat16)], axis=1
    )
    size = HEADS_PER_PASS * rows
    own = lax.broadcasted_iota(jnp.int32, (size, rows), 0) % rows
    one_hot = (own == lax.broadcasted_iota(jnp.int32, (size, rows), 1)).astype(jnp.bfloat16)

    def score(step):
        queries = jnp.concatenate([query_ref[step * size : (step + 1) * size, :], one_hot], axis=1)
        return lax.dot_general(
            queries, keys, (((1,), (1,)), ((), ())), preferred_element_type=jnp.float32
        )

    steps = query_ref.shape[0] // size
    following = score(0)
    for step in range(steps):
        scores = following
        if step + 1 < steps:
            following = score(step + 1)
        highest = jnp.max(scores, axis=-1, keepdims=True)
        weights = jnp.exp2((scores - highest) * SCALE).astype(jnp.bfloat16)
        summed = lax.dot_general(
            weights, values, (((1,), (0,)), ((), ())), preferred_element_type=jnp.float32
        )
        attended = (summed[:, :HEAD_DIM] / summed[:, HEAD_DIM:]).astype(jnp.bfloat16)
        for i in range(HEADS_PER_PASS):
            head = step * HEADS_PER_PASS + i
            out_ref[:, head * HEAD_DIM : (head + 1) * HEAD_DIM] = attended[
                i * rows : (i + 1) * rows
            ]


def attend(queries, gathered, mask, so_far, group, group_count):
    tokens, rows = mask.shape
    per_group = queries.shape[0] // group_count
    width = per_group // rows * HEAD_DIM
    in_specs = [
        pl.BlockSpec((per_group, HEAD_DIM), lambda i: (group, 0)),
        pl.BlockSpec(gathered.shape, lambda i: (0, 0, 0)),
        pl.BlockSpec(mask.shape, lambda i: (0, 0)),
    ]
    operands = [queries, gathered, mask]
    aliases = {}
    if so_far is not None:
        in_specs.append(pl.BlockSpec(memory_space=pl.ANY))
        operands.append(so_far)
        aliases = {3: 0}
    products = 4 * per_group * tokens * 2 * HEAD_DIM
    return pl.pallas_call(
        attend_kernel,
        grid=(1,),
        in_specs=in_specs,
        out_specs=pl.BlockSpec((rows, width), lambda i: (0, group)),
        out_shape=jax.ShapeDtypeStruct((rows, width * group_count), jnp.bfloat16),
        input_output_aliases=aliases,
        compiler_params=pltpu.CompilerParams(vmem_limit_bytes=40 * 1024 * 1024),
        cost_estimate=pl.CostEstimate(
            flops=products, bytes_accessed=2 * per_group * HEAD_DIM * 2, transcendentals=per_group * tokens
        ),
        name="attend",
    )(*operands)


def per_device(query_rows, key_rows, value_rows, positions):
    local_rows = query_rows.shape[1]
    key_heads = key_rows.shape[2] // HEAD_DIM
    owners = lax.axis_size("ctx")
    key_in, value_in = shifted((key_rows, value_rows), "section", 1)
    position_table = positions[0]
    own_pos = lax.dynamic_slice_in_dim(
        position_table, lax.axis_index("ctx") * local_rows, local_rows
    )
    cosine, sine = turn_tables(own_pos)
    mask = jnp.where(position_table[:, None] <= own_pos[None, :], 0.0, MASKED).astype(jnp.bfloat16)
    query_rows, cosine, sine = lax.optimization_barrier((query_rows, cosine, sine))
    query_in = shifted(query_rows, "section", 1)
    pieces = spread(key_in[0], value_in[0], cosine, sine, owners)
    gathered = [lax.all_to_all(piece, "ctx", 0, 0, tiled=False) for piece in pieces]
    queries = turn_queries(query_in[0], cosine, sine)
    result = None
    for group in range(key_heads):
        result = attend(queries, gathered[group], mask, result, group, key_heads)
    return result[None]


def solution(mesh):
    return jax.shard_map(
        per_device,
        mesh=mesh,
        in_specs=(
            P("section", "ctx", "tp"),
            P("section", "ctx", "tp"),
            P("section", "ctx", "tp"),
            P("section", None),
        ),
        out_specs=P("section", "ctx", "tp"),
        check_vma=False,
    )
```

```python
from functools import partial
import math

import jax
import jax.numpy as jnp
import numpy as np
from jax import lax
from jax.experimental import pallas as pl
from jax.experimental.pallas import tpu as pltpu
from jax.sharding import PartitionSpec as P

HEAD_DIM = 128
MASKED = -1e30
SCALE = math.log2(math.e) / math.sqrt(HEAD_DIM)
HEADS_PER_PASS = 2


def shifted(block, axis, distance):
    devices = range(lax.axis_size(axis))
    route = [((i - distance) % len(devices), i) for i in devices]
    return lax.ppermute(block, axis, route)


def rope_tables(head_size):
    index_ids = np.arange(head_size // 2) * 1.0
    natural = 500000.0 ** (-2.0 * index_ids / head_size)
    wavelength = 2.0 * math.pi / natural
    smooth = (8192.0 / wavelength - 1.0) / 3.0
    blended = (1.0 - smooth) * natural / 8.0 + smooth * natural
    scaled = np.where(
        wavelength < 2048.0, natural, np.where(wavelength > 8192.0, natural / 8.0, blended)
    )
    coarse = np.mod(1024.0 * scaled, 2.0 * math.pi)
    return (jnp.asarray(scaled, jnp.float32), jnp.asarray(coarse, jnp.float32))


def turn_tables(token_pos):
    fine_freq, coarse = rope_tables(HEAD_DIM)
    upper_part = (token_pos // 1024).astype(jnp.float32)
    lower_part = (token_pos % 1024).astype(jnp.float32)
    angles = upper_part[:, None] * coarse[None, :] + lower_part[:, None] * fine_freq[None, :]
    cosine, sine = jnp.cos(angles), jnp.sin(angles)
    return (
        jnp.concatenate([cosine, cosine], axis=-1),
        jnp.concatenate([-sine, sine], axis=-1),
    )


def turned(head, cosine, sine):
    head = head.astype(jnp.float32)
    return (head * cosine + pltpu.roll(head, HEAD_DIM // 2, 1) * sine).astype(jnp.bfloat16)


def spread_kernel(key_ref, value_ref, cosine_ref, sine_ref, out_ref):
    cosine, sine = cosine_ref[...], sine_ref[...]
    for head in range(key_ref.shape[1] // HEAD_DIM):
        columns = pl.ds(head * HEAD_DIM, HEAD_DIM)
        keys = turned(key_ref[:, columns], cosine, sine)
        values = value_ref[:, columns]
        for owner in range(out_ref.shape[0]):
            out_ref[owner, :, pl.ds(2 * head * HEAD_DIM, HEAD_DIM)] = keys
            out_ref[owner, :, pl.ds((2 * head + 1) * HEAD_DIM, HEAD_DIM)] = values


WHOLE = pl.BlockSpec(memory_space=pltpu.VMEM)


def spread(key_in, value_in, cosine, sine, owners):
    rows, width = key_in.shape
    return pl.pallas_call(
        spread_kernel,
        in_specs=[WHOLE] * 4,
        out_specs=WHOLE,
        out_shape=jax.ShapeDtypeStruct((owners, rows, 2 * width), jnp.bfloat16),
        name="spread",
    )(key_in, value_in, cosine, sine)


def turn_kernel(query_ref, cosine_ref, sine_ref, out_ref):
    cosine, sine = cosine_ref[...], sine_ref[...]
    rows = query_ref.shape[0]
    for head in range(query_ref.shape[1] // HEAD_DIM):
        out_ref[head * rows : (head + 1) * rows, :] = turned(
            query_ref[:, head * HEAD_DIM : (head + 1) * HEAD_DIM], cosine, sine
        )


def turn_queries(query_in, cosine, sine):
    rows, width = query_in.shape
    heads = width // HEAD_DIM
    return pl.pallas_call(
        turn_kernel,
        in_specs=[WHOLE] * 3,
        out_specs=WHOLE,
        out_shape=jax.ShapeDtypeStruct((heads * rows, HEAD_DIM), jnp.bfloat16),
        name="turn",
    )(query_in, cosine, sine)


def attend_kernel(raw_ref, cosine_ref, sine_ref, gathered_ref, mask_ref, out_ref, held_ref, query_ref, sent):
    turn_kernel(raw_ref, cosine_ref, sine_ref, query_ref)
    tokens, rows = mask_ref.shape
    key_heads = gathered_ref.shape[2] // (2 * HEAD_DIM)
    size = HEADS_PER_PASS * rows
    per_head = query_ref.shape[0] // key_heads
    own = lax.broadcasted_iota(jnp.int32, (size, rows), 0) % rows
    one_hot = (own == lax.broadcasted_iota(jnp.int32, (size, rows), 1)).astype(jnp.bfloat16)
    mask = mask_ref[...]
    ones = jnp.ones((tokens, HEAD_DIM), jnp.bfloat16)

    def part(index):
        piece = gathered_ref[:, :, index * HEAD_DIM : (index + 1) * HEAD_DIM]
        return piece.reshape(tokens, HEAD_DIM)

    def score(keys, step):
        queries = jnp.concatenate([query_ref[step * size : (step + 1) * size, :], one_hot], axis=1)
        return lax.dot_general(
            queries, keys, (((1,), (1,)), ((), ())), preferred_element_type=jnp.float32
        )

    copies = []
    steps = per_head // size
    for key_head in range(key_heads):
        keys = jnp.concatenate([part(2 * key_head), mask], axis=1)
        values = jnp.concatenate([part(2 * key_head + 1), ones], axis=1)
        following = score(keys, key_head * steps)
        for step in range(key_head * steps, (key_head + 1) * steps):
            scores = following
            if step + 1 < (key_head + 1) * steps:
                following = score(keys, step + 1)
            highest = jnp.max(scores, axis=-1, keepdims=True)
            weights = jnp.exp2((scores - highest) * SCALE).astype(jnp.bfloat16)
            summed = lax.dot_general(
                weights, values, (((1,), (0,)), ((), ())), preferred_element_type=jnp.float32
            )
            attended = (summed[:, :HEAD_DIM] / summed[:, HEAD_DIM:]).astype(jnp.bfloat16)
            for i in range(HEADS_PER_PASS):
                head = step * HEADS_PER_PASS + i
                held_ref[:, head * HEAD_DIM : (head + 1) * HEAD_DIM] = attended[
                    i * rows : (i + 1) * rows
                ]
            columns = pl.ds(step * HEADS_PER_PASS * HEAD_DIM, HEADS_PER_PASS * HEAD_DIM)
            copies.append(
                pltpu.make_async_copy(held_ref.at[:, columns], out_ref.at[:, columns], sent.at[step])
            )
            copies[-1].start()
    for copy in copies:
        copy.wait()


def attend(queries, cosine, sine, gathered, mask):
    tokens, rows = mask.shape
    heads = queries.shape[1] // HEAD_DIM
    return pl.pallas_call(
        attend_kernel,
        in_specs=[WHOLE] * 5,
        out_specs=pl.BlockSpec(memory_space=pl.ANY),
        out_shape=jax.ShapeDtypeStruct((rows, heads * HEAD_DIM), jnp.bfloat16),
        scratch_shapes=[
            pltpu.VMEM((rows, heads * HEAD_DIM), jnp.bfloat16),
            pltpu.VMEM((rows * heads, HEAD_DIM), jnp.bfloat16),
            pltpu.SemaphoreType.DMA((heads // HEADS_PER_PASS,)),
        ],
        compiler_params=pltpu.CompilerParams(vmem_limit_bytes=40 * 1024 * 1024),
        cost_estimate=pl.CostEstimate(
            flops=8 * heads * rows * tokens * HEAD_DIM,
            bytes_accessed=4 * heads * rows * HEAD_DIM,
            transcendentals=heads * rows * tokens,
        ),
        name="attend",
    )(queries, cosine, sine, gathered, mask)


def per_device(query_rows, key_rows, value_rows, positions):
    local_rows = query_rows.shape[1]
    key_heads = key_rows.shape[2] // HEAD_DIM
    owners = lax.axis_size("ctx")
    key_in, value_in = shifted((key_rows, value_rows), "section", 1)
    position_table = positions[0]
    own_pos = lax.dynamic_slice_in_dim(
        position_table, lax.axis_index("ctx") * local_rows, local_rows
    )
    cosine, sine = turn_tables(own_pos)
    mask = jnp.where(position_table[:, None] <= own_pos[None, :], 0.0, MASKED).astype(jnp.bfloat16)
    query_rows, own_pos = lax.optimization_barrier((query_rows, own_pos))
    query_in = shifted(query_rows, "section", 1)
    spread_rows = spread(key_in[0], value_in[0], cosine, sine, owners)
    gathered = lax.all_to_all(spread_rows, "ctx", 0, 0, tiled=False)
    return attend(query_in[0], cosine, sine, gathered, mask)[None]


def solution(mesh):
    return jax.shard_map(
        per_device,
        mesh=mesh,
        in_specs=(
            P("section", "ctx", "tp"),
            P("section", "ctx", "tp"),
            P("section", "ctx", "tp"),
            P("section", None),
        ),
        out_specs=P("section", "ctx", "tp"),
        check_vma=False,
    )
```

```python
from functools import partial
import math

import jax
import jax.numpy as jnp
import numpy as np
from jax import lax
from jax.experimental import pallas as pl
from jax.experimental.pallas import tpu as pltpu
from jax.sharding import PartitionSpec as P

HEAD_DIM = 128
MASKED = -1e30
SCALE = math.log2(math.e) / math.sqrt(HEAD_DIM)
HEADS_PER_PASS = 4
GROUPS = ((0, 1, 2), (3,))


def shifted(block, axis, distance):
    devices = range(lax.axis_size(axis))
    route = [((i - distance) % len(devices), i) for i in devices]
    return lax.ppermute(block, axis, route)


def rope_tables():
    index_ids = np.arange(HEAD_DIM // 2) * 1.0
    natural = 500000.0 ** (-2.0 * index_ids / HEAD_DIM)
    wavelength = 2.0 * math.pi / natural
    smooth = (8192.0 / wavelength - 1.0) / 3.0
    blended = (1.0 - smooth) * natural / 8.0 + smooth * natural
    scaled = np.where(
        wavelength < 2048.0, natural, np.where(wavelength > 8192.0, natural / 8.0, blended)
    )
    coarse = np.mod(1024.0 * scaled, 2.0 * math.pi)
    sign = np.repeat(np.array([-1.0, 1.0]), HEAD_DIM // 2)
    return [jnp.asarray(table, jnp.float32) for table in (np.tile(scaled, 2), np.tile(coarse, 2), sign)]


def turn_tables(token_pos):
    fine, coarse, sign = rope_tables()
    upper_part = (token_pos // 1024).astype(jnp.float32)
    lower_part = (token_pos % 1024).astype(jnp.float32)
    angles = upper_part[:, None] * coarse[None, :] + lower_part[:, None] * fine[None, :]
    return jnp.cos(angles), jnp.sin(angles) * sign[None, :]


def turned(head, cosine, sine):
    head = head.astype(jnp.float32)
    return (head * cosine + pltpu.roll(head, HEAD_DIM // 2, 1) * sine).astype(jnp.bfloat16)


def turned_rows(rows, cosine, sine):
    half = rows.shape[1] // 2
    heads = [turned(rows[:, i : i + HEAD_DIM], cosine, sine) for i in range(0, half, HEAD_DIM)]
    return jnp.concatenate(heads + [rows[:, half:]], axis=1)


def turn_pair_kernel(own_ref, partner_ref, cosine_ref, sine_ref, out_ref):
    count = own_ref.shape[0]
    for i, ref in enumerate((own_ref, partner_ref)):
        place = pl.ds(i * count, count)
        out_ref[place] = turned_rows(ref[...], cosine_ref[place], sine_ref[place])


WHOLE = pl.BlockSpec(memory_space=pltpu.VMEM)
SMALL = pltpu.CompilerParams(vmem_limit_bytes=8 * 1024 * 1024)


def turn_pair(own_rows, partner_rows, cosine, sine):
    rows, width = own_rows.shape
    return pl.pallas_call(
        turn_pair_kernel,
        in_specs=[WHOLE] * 4,
        out_specs=WHOLE,
        out_shape=jax.ShapeDtypeStruct((2 * rows, width), jnp.bfloat16),
        compiler_params=SMALL,
        name="turn_pair",
    )(own_rows, partner_rows, cosine, sine)


def turn_kernel(query_ref, cosine_ref, sine_ref, out_ref):
    rows = query_ref.shape[0]
    cosine, sine = cosine_ref[:rows], sine_ref[:rows]
    for head in range(query_ref.shape[1] // HEAD_DIM):
        out_ref[head * rows : (head + 1) * rows, :] = turned(
            query_ref[:, head * HEAD_DIM : (head + 1) * HEAD_DIM], cosine, sine
        )


def turn_queries(query_in, cosine, sine):
    rows, width = query_in.shape
    heads = width // HEAD_DIM
    return pl.pallas_call(
        turn_kernel,
        in_specs=[WHOLE] * 3,
        out_specs=WHOLE,
        out_shape=jax.ShapeDtypeStruct((heads * rows, HEAD_DIM), jnp.bfloat16),
        compiler_params=pltpu.CompilerParams(vmem_limit_bytes=8 * 1024 * 1024),
        name="turn",
    )(query_in, cosine, sine)


def attend_kernel(*refs, pieces, first, last):
    refs = list(refs)
    query_ref, *piece_refs = refs[: 1 + pieces]
    mask_ref = refs[1 + pieces]
    refs = refs[2 + pieces :]
    if not first:
        before_ref, before_highest_ref = refs[:2]
        refs = refs[2:]
    if last:
        out_ref, held_ref, sent = refs
    else:
        sums_ref, highest_ref = refs
    tokens, rows = mask_ref.shape
    key_heads = piece_refs[0].shape[1] // (2 * HEAD_DIM)
    size = HEADS_PER_PASS * rows
    steps = query_ref.shape[0] // key_heads // size
    own = lax.broadcasted_iota(jnp.int32, (size, rows), 0) % rows
    one_hot = (own == lax.broadcasted_iota(jnp.int32, (size, rows), 1)).astype(jnp.bfloat16)
    mask = mask_ref[...]
    ones = jnp.ones((tokens, HEAD_DIM), jnp.bfloat16)

    def part(index):
        columns = pl.ds(index * HEAD_DIM, HEAD_DIM)
        return jnp.concatenate([ref[:, columns] for ref in piece_refs], axis=0)

    def score(keys, step):
        queries = jnp.concatenate([query_ref[step * size : (step + 1) * size, :], one_hot], axis=1)
        return lax.dot_general(
            queries, keys, (((1,), (1,)), ((), ())), preferred_element_type=jnp.float32
        )

    copies = []
    for key_head in range(key_heads):
        keys = jnp.concatenate([part(key_head), mask], axis=1)
        values = jnp.concatenate([part(key_heads + key_head), ones], axis=1)
        following = score(keys, key_head * steps)
        for step in range(key_head * steps, (key_head + 1) * steps):
            place = pl.ds(step * size, size)
            scores = following
            if step + 1 < (key_head + 1) * steps:
                following = score(keys, step + 1)
            highest = jnp.max(scores, axis=-1, keepdims=True)
            if not first:
                before = before_highest_ref[place][:, :1]
                highest = jnp.maximum(highest, before)
            weights = jnp.exp2((scores - highest) * SCALE).astype(jnp.bfloat16)
            summed = lax.dot_general(
                weights, values, (((1,), (0,)), ((), ())), preferred_element_type=jnp.float32
            )
            if not first:
                summed = summed + before_ref[place] * jnp.exp2((before - highest) * SCALE)
            if not last:
                sums_ref[place] = summed
                highest_ref[place] = jnp.broadcast_to(highest, (size, HEAD_DIM))
                continue
            attended = (summed[:, :HEAD_DIM] / summed[:, HEAD_DIM:]).astype(jnp.bfloat16)
            for i in range(HEADS_PER_PASS):
                head = step * HEADS_PER_PASS + i
                held_ref[:, head * HEAD_DIM : (head + 1) * HEAD_DIM] = attended[
                    i * rows : (i + 1) * rows
                ]
            columns = pl.ds(step * HEADS_PER_PASS * HEAD_DIM, HEADS_PER_PASS * HEAD_DIM)
            copies.append(
                pltpu.make_async_copy(held_ref.at[:, columns], out_ref.at[:, columns], sent.at[step])
            )
            copies[-1].start()
    for copy in copies:
        copy.wait()


def attend(queries, pieces, mask, carried, last):
    tokens, rows = mask.shape
    count = queries.shape[0]
    heads = count // rows
    if last:
        out_specs = pl.BlockSpec(memory_space=pl.ANY)
        out_shape = jax.ShapeDtypeStruct((rows, heads * HEAD_DIM), jnp.bfloat16)
        scratch = [
            pltpu.VMEM((rows, heads * HEAD_DIM), jnp.bfloat16),
            pltpu.SemaphoreType.DMA((heads // HEADS_PER_PASS,)),
        ]
    else:
        out_specs = [WHOLE] * 2
        out_shape = [
            jax.ShapeDtypeStruct((count, 2 * HEAD_DIM), jnp.float32),
            jax.ShapeDtypeStruct((count, HEAD_DIM), jnp.float32),
        ]
        scratch = []
    operands = [queries, *pieces, mask, *carried]
    return pl.pallas_call(
        partial(attend_kernel, pieces=len(pieces), first=not carried, last=last),
        in_specs=[WHOLE] * len(operands),
        out_specs=out_specs,
        out_shape=out_shape,
        scratch_shapes=scratch,
        compiler_params=pltpu.CompilerParams(vmem_limit_bytes=24 * 1024 * 1024),
        cost_estimate=pl.CostEstimate(flops=1000, bytes_accessed=1000, transcendentals=0),
        name="attend",
    )(*operands)


def per_device(query_rows, key_rows, value_rows, positions):
    local_rows = query_rows.shape[1]
    sections, owners = lax.axis_size("section"), lax.axis_size("ctx")
    rows = jnp.concatenate([key_rows[0], value_rows[0]], axis=1)
    own_rows = shifted(rows, "section", 1)
    partner_rows = lax.ppermute(
        rows,
        ("section", "ctx"),
        [
            ((s - 1) % sections * owners + (c ^ 1), s * owners + c)
            for s in range(sections)
            for c in range(owners)
        ],
    )
    owner_index = lax.axis_index("ctx")
    blocks = positions[0].reshape(owners, local_rows)

    def pair_pos(index):
        return [lax.dynamic_index_in_dim(blocks, i, keepdims=False) for i in (index, index ^ 1)]

    def beside(index, hop):
        return (index + (1 - index % 2 * 2) * hop) % owners

    def route(hop):
        return [(beside(c, hop), c) for c in range(owners)]

    key_pos = [pair_pos(beside(owner_index, hop)) for hop in (0, 2, -1, -3)]
    own_pos = key_pos[0][0]
    cosine, sine = turn_tables(jnp.concatenate(key_pos[0]))
    masks = [
        jnp.where(jnp.concatenate(pos)[:, None] <= own_pos[None, :], 0.0, MASKED).astype(jnp.bfloat16)
        for pos in key_pos
    ]
    pair_rows = turn_pair(own_rows, partner_rows, cosine, sine)
    query_rows, pair_rows = lax.optimization_barrier((query_rows, pair_rows))
    query_in = shifted(query_rows, "section", 1)
    second = lax.ppermute(pair_rows, "ctx", route(2))
    beside_rows = lax.ppermute(pair_rows, "ctx", route(-1))
    across = lax.ppermute(second, "ctx", route(-1))
    queries = turn_queries(query_in[0], cosine, sine)
    carried = ()
    for i, pieces in enumerate(GROUPS):
        last = i + 1 == len(GROUPS)
        arrived = [(pair_rows, second, beside_rows, across)[p] for p in pieces]
        mask = jnp.concatenate([masks[p] for p in pieces], axis=0)
        carried = attend(queries, arrived, mask, carried, last)
    return carried[None]


def solution(mesh):
    return jax.shard_map(
        per_device,
        mesh=mesh,
        in_specs=(
            P("section", "ctx", "tp"),
            P("section", "ctx", "tp"),
            P("section", "ctx", "tp"),
            P("section", None),
        ),
        out_specs=P("section", "ctx", "tp"),
        check_vma=False,
    )
```

```python
from functools import partial
import math

import jax
import jax.numpy as jnp
import numpy as np
from jax import lax
from jax.experimental import pallas as pl
from jax.experimental.pallas import tpu as pltpu
from jax.sharding import PartitionSpec as P

HEAD_DIM = 128
MASKED = -1e30
SCALE = math.log2(math.e) / math.sqrt(HEAD_DIM)
HEADS_PER_PASS = 4
GROUPS = ((0,), (1, 2), (3,))


def shifted(block, axis, distance):
    devices = range(lax.axis_size(axis))
    route = [((i - distance) % len(devices), i) for i in devices]
    return lax.ppermute(block, axis, route)


def rope_tables():
    index_ids = np.arange(HEAD_DIM // 2) * 1.0
    natural = 500000.0 ** (-2.0 * index_ids / HEAD_DIM)
    wavelength = 2.0 * math.pi / natural
    smooth = (8192.0 / wavelength - 1.0) / 3.0
    blended = (1.0 - smooth) * natural / 8.0 + smooth * natural
    scaled = np.where(
        wavelength < 2048.0, natural, np.where(wavelength > 8192.0, natural / 8.0, blended)
    )
    coarse = np.mod(1024.0 * scaled, 2.0 * math.pi)
    sign = np.repeat(np.array([-1.0, 1.0]), HEAD_DIM // 2)
    return [jnp.asarray(table, jnp.float32) for table in (np.tile(scaled, 2), np.tile(coarse, 2), sign)]


def turn_tables(token_pos):
    fine, coarse, sign = rope_tables()
    upper_part = (token_pos // 1024).astype(jnp.float32)
    lower_part = (token_pos % 1024).astype(jnp.float32)
    angles = upper_part[:, None] * coarse[None, :] + lower_part[:, None] * fine[None, :]
    return jnp.cos(angles), jnp.sin(angles) * sign[None, :]


def turned(head, cosine, sine):
    head = head.astype(jnp.float32)
    return (head * cosine + pltpu.roll(head, HEAD_DIM // 2, 1) * sine).astype(jnp.bfloat16)


def turned_rows(rows, cosine, sine):
    half = rows.shape[1] // 2
    heads = [turned(rows[:, i : i + HEAD_DIM], cosine, sine) for i in range(0, half, HEAD_DIM)]
    return jnp.concatenate(heads + [rows[:, half:]], axis=1)


def turn_pair_kernel(own_ref, partner_ref, cosine_ref, sine_ref, out_ref):
    count = own_ref.shape[0]
    for i, ref in enumerate((own_ref, partner_ref)):
        place = pl.ds(i * count, count)
        out_ref[place] = turned_rows(ref[...], cosine_ref[place], sine_ref[place])


WHOLE = pl.BlockSpec(memory_space=pltpu.VMEM)
SMALL = pltpu.CompilerParams(vmem_limit_bytes=8 * 1024 * 1024)


def turn_pair(own_rows, partner_rows, cosine, sine):
    rows, width = own_rows.shape
    return pl.pallas_call(
        turn_pair_kernel,
        in_specs=[WHOLE] * 4,
        out_specs=WHOLE,
        out_shape=jax.ShapeDtypeStruct((2 * rows, width), jnp.bfloat16),
        compiler_params=SMALL,
        name="turn_pair",
    )(own_rows, partner_rows, cosine, sine)


def turn_kernel(query_ref, cosine_ref, sine_ref, out_ref):
    rows = query_ref.shape[0]
    cosine, sine = cosine_ref[:rows], sine_ref[:rows]
    for head in range(query_ref.shape[1] // HEAD_DIM):
        out_ref[head * rows : (head + 1) * rows, :] = turned(
            query_ref[:, head * HEAD_DIM : (head + 1) * HEAD_DIM], cosine, sine
        )


def turn_queries(query_in, cosine, sine):
    rows, width = query_in.shape
    heads = width // HEAD_DIM
    return pl.pallas_call(
        turn_kernel,
        in_specs=[WHOLE] * 3,
        out_specs=WHOLE,
        out_shape=jax.ShapeDtypeStruct((heads * rows, HEAD_DIM), jnp.bfloat16),
        compiler_params=pltpu.CompilerParams(vmem_limit_bytes=8 * 1024 * 1024),
        name="turn",
    )(query_in, cosine, sine)


def attend_kernel(*refs, pieces, first, last):
    refs = list(refs)
    query_ref, *piece_refs = refs[: 1 + pieces]
    mask_ref = refs[1 + pieces]
    refs = refs[2 + pieces :]
    if not first:
        before_ref, before_highest_ref = refs[:2]
        refs = refs[2:]
    if last:
        out_ref, held_ref, sent = refs
    else:
        sums_ref, highest_ref = refs
    tokens, rows = mask_ref.shape
    key_heads = piece_refs[0].shape[1] // (2 * HEAD_DIM)
    size = HEADS_PER_PASS * rows
    steps = query_ref.shape[0] // key_heads // size
    own = lax.broadcasted_iota(jnp.int32, (size, rows), 0) % rows
    one_hot = (own == lax.broadcasted_iota(jnp.int32, (size, rows), 1)).astype(jnp.bfloat16)
    mask = mask_ref[...]
    ones = jnp.ones((tokens, HEAD_DIM), jnp.bfloat16)

    def part(index):
        columns = pl.ds(index * HEAD_DIM, HEAD_DIM)
        return jnp.concatenate([ref[:, columns] for ref in piece_refs], axis=0)

    def score(keys, step):
        queries = jnp.concatenate([query_ref[step * size : (step + 1) * size, :], one_hot], axis=1)
        return lax.dot_general(
            queries, keys, (((1,), (1,)), ((), ())), preferred_element_type=jnp.float32
        )

    copies = []
    for key_head in range(key_heads):
        keys = jnp.concatenate([part(key_head), mask], axis=1)
        values = jnp.concatenate([part(key_heads + key_head), ones], axis=1)
        following = score(keys, key_head * steps)
        for step in range(key_head * steps, (key_head + 1) * steps):
            place = pl.ds(step * size, size)
            scores = following
            if step + 1 < (key_head + 1) * steps:
                following = score(keys, step + 1)
            highest = jnp.broadcast_to(jnp.max(scores, axis=-1, keepdims=True), (size, HEAD_DIM))
            if not first:
                before = before_highest_ref[place]
                highest = jnp.maximum(highest, before)
            weights = jnp.concatenate(
                [
                    jnp.exp2((scores[:, i : i + HEAD_DIM] - highest) * SCALE).astype(jnp.bfloat16)
                    for i in range(0, tokens, HEAD_DIM)
                ],
                axis=1,
            )
            summed = lax.dot_general(
                weights, values, (((1,), (0,)), ((), ())), preferred_element_type=jnp.float32
            )
            if not first:
                factor = jnp.exp2((before - highest) * SCALE)
                summed = summed + before_ref[place] * jnp.concatenate([factor, factor], axis=1)
            if not last:
                sums_ref[place] = summed
                highest_ref[place] = highest
                continue
            attended = (summed[:, :HEAD_DIM] / summed[:, HEAD_DIM:]).astype(jnp.bfloat16)
            for i in range(HEADS_PER_PASS):
                head = step * HEADS_PER_PASS + i
                held_ref[:, head * HEAD_DIM : (head + 1) * HEAD_DIM] = attended[
                    i * rows : (i + 1) * rows
                ]
            columns = pl.ds(step * HEADS_PER_PASS * HEAD_DIM, HEADS_PER_PASS * HEAD_DIM)
            copies.append(
                pltpu.make_async_copy(held_ref.at[:, columns], out_ref.at[:, columns], sent.at[step])
            )
            copies[-1].start()
    for copy in copies:
        copy.wait()


def attend(queries, pieces, mask, carried, last):
    tokens, rows = mask.shape
    count = queries.shape[0]
    heads = count // rows
    if last:
        out_specs = pl.BlockSpec(memory_space=pl.ANY)
        out_shape = jax.ShapeDtypeStruct((rows, heads * HEAD_DIM), jnp.bfloat16)
        scratch = [
            pltpu.VMEM((rows, heads * HEAD_DIM), jnp.bfloat16),
            pltpu.SemaphoreType.DMA((heads // HEADS_PER_PASS,)),
        ]
    else:
        out_specs = [WHOLE] * 2
        out_shape = [
            jax.ShapeDtypeStruct((count, 2 * HEAD_DIM), jnp.float32),
            jax.ShapeDtypeStruct((count, HEAD_DIM), jnp.float32),
        ]
        scratch = []
    operands = [queries, *pieces, mask, *carried]
    return pl.pallas_call(
        partial(attend_kernel, pieces=len(pieces), first=not carried, last=last),
        in_specs=[WHOLE] * len(operands),
        out_specs=out_specs,
        out_shape=out_shape,
        scratch_shapes=scratch,
        compiler_params=pltpu.CompilerParams(vmem_limit_bytes=24 * 1024 * 1024),
        cost_estimate=pl.CostEstimate(flops=1000, bytes_accessed=1000, transcendentals=0),
        name="attend",
    )(*operands)


def per_device(query_rows, key_rows, value_rows, positions):
    local_rows = query_rows.shape[1]
    sections, owners = lax.axis_size("section"), lax.axis_size("ctx")
    rows = jnp.concatenate([key_rows[0], value_rows[0]], axis=1)
    own_rows = shifted(rows, "section", 1)
    partner_rows = lax.ppermute(
        rows,
        ("section", "ctx"),
        [
            ((s - 1) % sections * owners + (c ^ 1), s * owners + c)
            for s in range(sections)
            for c in range(owners)
        ],
    )
    owner_index = lax.axis_index("ctx")
    blocks = positions[0].reshape(owners, local_rows)

    def pair_pos(index):
        return [lax.dynamic_index_in_dim(blocks, i, keepdims=False) for i in (index, index ^ 1)]

    def beside(index, hop):
        return (index + (1 - index % 2 * 2) * hop) % owners

    def route(hop):
        return [(beside(c, hop), c) for c in range(owners)]

    key_pos = [pair_pos(beside(owner_index, hop)) for hop in (0, 2, -1, -3)]
    own_pos = key_pos[0][0]
    cosine, sine = turn_tables(jnp.concatenate(key_pos[0]))
    masks = [
        jnp.where(jnp.concatenate(pos)[:, None] <= own_pos[None, :], 0.0, MASKED).astype(jnp.bfloat16)
        for pos in key_pos
    ]
    query_rows, own_rows = lax.optimization_barrier((query_rows, own_rows))
    query_in = shifted(query_rows, "section", 1)
    pair_rows = turn_pair(own_rows, partner_rows, cosine, sine)
    second = lax.ppermute(pair_rows, "ctx", route(2))
    beside_rows = lax.ppermute(pair_rows, "ctx", route(-1))
    across = lax.ppermute(second, "ctx", route(-1))
    queries = turn_queries(query_in[0], cosine, sine)
    carried = ()
    for i, pieces in enumerate(GROUPS):
        last = i + 1 == len(GROUPS)
        arrived = [(pair_rows, second, beside_rows, across)[p] for p in pieces]
        mask = jnp.concatenate([masks[p] for p in pieces], axis=0)
        carried = attend(queries, arrived, mask, carried, last)
    return carried[None]


def solution(mesh):
    return jax.shard_map(
        per_device,
        mesh=mesh,
        in_specs=(
            P("section", "ctx", "tp"),
            P("section", "ctx", "tp"),
            P("section", "ctx", "tp"),
            P("section", None),
        ),
        out_specs=P("section", "ctx", "tp"),
        check_vma=False,
    )
```

```python
from functools import partial
import math

import jax
import jax.numpy as jnp
import numpy as np
from jax import lax
from jax.experimental import pallas as pl
from jax.experimental.pallas import tpu as pltpu
from jax.sharding import PartitionSpec as P

HEAD_DIM = 128
MASKED = -1e30
SCALE = math.log2(math.e) / math.sqrt(HEAD_DIM)
HEADS_PER_PASS = 4
GROUPS = ((0, 1, 2), (3,))


def shifted(block, axis, distance):
    devices = range(lax.axis_size(axis))
    route = [((i - distance) % len(devices), i) for i in devices]
    return lax.ppermute(block, axis, route)


def rope_tables():
    index_ids = np.arange(HEAD_DIM // 2) * 1.0
    natural = 500000.0 ** (-2.0 * index_ids / HEAD_DIM)
    wavelength = 2.0 * math.pi / natural
    smooth = (8192.0 / wavelength - 1.0) / 3.0
    blended = (1.0 - smooth) * natural / 8.0 + smooth * natural
    scaled = np.where(
        wavelength < 2048.0, natural, np.where(wavelength > 8192.0, natural / 8.0, blended)
    )
    coarse = np.mod(1024.0 * scaled, 2.0 * math.pi)
    sign = np.repeat(np.array([-1.0, 1.0]), HEAD_DIM // 2)
    return [jnp.asarray(table, jnp.float32) for table in (np.tile(scaled, 2), np.tile(coarse, 2), sign)]


def turn_tables(token_pos):
    fine, coarse, sign = rope_tables()
    upper_part = (token_pos // 1024).astype(jnp.float32)
    lower_part = (token_pos % 1024).astype(jnp.float32)
    angles = upper_part[:, None] * coarse[None, :] + lower_part[:, None] * fine[None, :]
    return jnp.cos(angles), jnp.sin(angles) * sign[None, :]


def turned(head, cosine, sine):
    head = head.astype(jnp.float32)
    return (head * cosine + pltpu.roll(head, HEAD_DIM // 2, 1) * sine).astype(jnp.bfloat16)


def turned_rows(rows, cosine, sine):
    half = rows.shape[1] // 2
    heads = [turned(rows[:, i : i + HEAD_DIM], cosine, sine) for i in range(0, half, HEAD_DIM)]
    return jnp.concatenate(heads + [rows[:, half:]], axis=1)


def turn_pair_kernel(own_ref, partner_ref, cosine_ref, sine_ref, out_ref):
    count = own_ref.shape[0]
    for i, ref in enumerate((own_ref, partner_ref)):
        place = pl.ds(i * count, count)
        out_ref[place] = turned_rows(ref[...], cosine_ref[place], sine_ref[place])


WHOLE = pl.BlockSpec(memory_space=pltpu.VMEM)
SMALL = pltpu.CompilerParams(vmem_limit_bytes=8 * 1024 * 1024)


def turn_pair(own_rows, partner_rows, cosine, sine):
    rows, width = own_rows.shape
    return pl.pallas_call(
        turn_pair_kernel,
        in_specs=[WHOLE] * 4,
        out_specs=WHOLE,
        out_shape=jax.ShapeDtypeStruct((2 * rows, width), jnp.bfloat16),
        compiler_params=SMALL,
        name="turn_pair",
    )(own_rows, partner_rows, cosine, sine)


def turn_kernel(query_ref, cosine_ref, sine_ref, out_ref):
    rows = query_ref.shape[0]
    cosine, sine = cosine_ref[:rows], sine_ref[:rows]
    for head in range(query_ref.shape[1] // HEAD_DIM):
        out_ref[head * rows : (head + 1) * rows, :] = turned(
            query_ref[:, head * HEAD_DIM : (head + 1) * HEAD_DIM], cosine, sine
        )


def turn_queries(query_in, cosine, sine):
    rows, width = query_in.shape
    heads = width // HEAD_DIM
    return pl.pallas_call(
        turn_kernel,
        in_specs=[WHOLE] * 3,
        out_specs=WHOLE,
        out_shape=jax.ShapeDtypeStruct((heads * rows, HEAD_DIM), jnp.bfloat16),
        compiler_params=pltpu.CompilerParams(vmem_limit_bytes=8 * 1024 * 1024),
        name="turn",
    )(query_in, cosine, sine)


def attend_kernel(*refs, pieces, first, last):
    refs = list(refs)
    query_ref, *piece_refs = refs[: 1 + pieces]
    mask_ref = refs[1 + pieces]
    refs = refs[2 + pieces :]
    if not first:
        before_ref, before_highest_ref = refs[:2]
        refs = refs[2:]
    if last:
        out_ref, held_ref, sent = refs
    else:
        sums_ref, highest_ref = refs
    tokens, rows = mask_ref.shape
    key_heads = piece_refs[0].shape[1] // (2 * HEAD_DIM)
    size = HEADS_PER_PASS * rows
    steps = query_ref.shape[0] // key_heads // size
    own = lax.broadcasted_iota(jnp.int32, (size, rows), 0) % rows
    one_hot = (own == lax.broadcasted_iota(jnp.int32, (size, rows), 1)).astype(jnp.bfloat16)
    mask = mask_ref[...]
    ones = jnp.ones((tokens, HEAD_DIM), jnp.bfloat16)

    def part(index):
        columns = pl.ds(index * HEAD_DIM, HEAD_DIM)
        return jnp.concatenate([ref[:, columns] for ref in piece_refs], axis=0)

    def score(keys, step):
        queries = jnp.concatenate([query_ref[step * size : (step + 1) * size, :], one_hot], axis=1)
        return lax.dot_general(
            queries, keys, (((1,), (1,)), ((), ())), preferred_element_type=jnp.float32
        )

    copies = []
    keys = [jnp.concatenate([part(i), mask], axis=1) for i in range(key_heads)]
    following = score(keys[0], 0)
    for key_head in range(key_heads):
        values = jnp.concatenate([part(key_heads + key_head), ones], axis=1)
        for step in range(key_head * steps, (key_head + 1) * steps):
            place = pl.ds(step * size, size)
            scores = following
            if step + 1 < key_heads * steps:
                following = score(keys[(step + 1) // steps], step + 1)
            highest = jnp.broadcast_to(jnp.max(scores, axis=-1, keepdims=True), (size, HEAD_DIM))
            if not first:
                before = before_highest_ref[place]
                highest = jnp.maximum(highest, before)
            weights = jnp.concatenate(
                [
                    jnp.exp2((scores[:, i : i + HEAD_DIM] - highest) * SCALE).astype(jnp.bfloat16)
                    for i in range(0, tokens, HEAD_DIM)
                ],
                axis=1,
            )
            summed = lax.dot_general(
                weights, values, (((1,), (0,)), ((), ())), preferred_element_type=jnp.float32
            )
            if not first:
                factor = jnp.exp2((before - highest) * SCALE)
                summed = summed + before_ref[place] * jnp.concatenate([factor, factor], axis=1)
            if not last:
                sums_ref[place] = summed
                highest_ref[place] = highest
                continue
            attended = (summed[:, :HEAD_DIM] / summed[:, HEAD_DIM:]).astype(jnp.bfloat16)
            first_column = step * HEADS_PER_PASS * HEAD_DIM
            held_ref[:, first_column : first_column + HEADS_PER_PASS * HEAD_DIM] = jnp.concatenate(
                [attended[i * rows : (i + 1) * rows] for i in range(HEADS_PER_PASS)], axis=1
            )
            columns = pl.ds(step * HEADS_PER_PASS * HEAD_DIM, HEADS_PER_PASS * HEAD_DIM)
            copies.append(
                pltpu.make_async_copy(held_ref.at[:, columns], out_ref.at[:, columns], sent.at[step])
            )
            copies[-1].start()
    for copy in copies:
        copy.wait()


def attend(queries, pieces, mask, carried, last):
    tokens, rows = mask.shape
    count = queries.shape[0]
    heads = count // rows
    if last:
        out_specs = pl.BlockSpec(memory_space=pl.ANY)
        out_shape = jax.ShapeDtypeStruct((rows, heads * HEAD_DIM), jnp.bfloat16)
        scratch = [
            pltpu.VMEM((rows, heads * HEAD_DIM), jnp.bfloat16),
            pltpu.SemaphoreType.DMA((heads // HEADS_PER_PASS,)),
        ]
    else:
        out_specs = [WHOLE] * 2
        out_shape = [
            jax.ShapeDtypeStruct((count, 2 * HEAD_DIM), jnp.float32),
            jax.ShapeDtypeStruct((count, HEAD_DIM), jnp.float32),
        ]
        scratch = []
    operands = [queries, *pieces, mask, *carried]
    return pl.pallas_call(
        partial(attend_kernel, pieces=len(pieces), first=not carried, last=last),
        in_specs=[WHOLE] * len(operands),
        out_specs=out_specs,
        out_shape=out_shape,
        scratch_shapes=scratch,
        compiler_params=pltpu.CompilerParams(vmem_limit_bytes=24 * 1024 * 1024),
        cost_estimate=pl.CostEstimate(flops=1000, bytes_accessed=1000, transcendentals=0),
        name="attend",
    )(*operands)


def per_device(query_rows, key_rows, value_rows, positions):
    local_rows = query_rows.shape[1]
    sections, owners = lax.axis_size("section"), lax.axis_size("ctx")
    rows = jnp.concatenate([key_rows[0], value_rows[0]], axis=1)
    own_rows = shifted(rows, "section", 1)
    partner_rows = lax.ppermute(
        rows,
        ("section", "ctx"),
        [
            ((s - 1) % sections * owners + (c ^ 1), s * owners + c)
            for s in range(sections)
            for c in range(owners)
        ],
    )
    owner_index = lax.axis_index("ctx")
    blocks = positions[0].reshape(owners, local_rows)

    def pair_pos(index):
        return [lax.dynamic_index_in_dim(blocks, i, keepdims=False) for i in (index, index ^ 1)]

    def beside(index, hop):
        return (index + (1 - index % 2 * 2) * hop) % owners

    def route(hop):
        return [(beside(c, hop), c) for c in range(owners)]

    key_pos = [pair_pos(beside(owner_index, hop)) for hop in (0, 2, -1, -3)]
    own_pos = key_pos[0][0]
    cosine, sine = turn_tables(jnp.concatenate(key_pos[0]))
    masks = [
        jnp.where(jnp.concatenate(pos)[:, None] <= own_pos[None, :], 0.0, MASKED).astype(jnp.bfloat16)
        for pos in key_pos
    ]
    query_rows, own_rows = lax.optimization_barrier((query_rows, own_rows))
    query_in = shifted(query_rows, "section", 1)
    pair_rows = turn_pair(own_rows, partner_rows, cosine, sine)
    second = lax.ppermute(pair_rows, "ctx", route(2))
    beside_rows = lax.ppermute(pair_rows, "ctx", route(-1))
    across = lax.ppermute(second, "ctx", route(-1))
    queries = turn_queries(query_in[0], cosine, sine)
    carried = ()
    for i, pieces in enumerate(GROUPS):
        last = i + 1 == len(GROUPS)
        arrived = [(pair_rows, second, beside_rows, across)[p] for p in pieces]
        mask = jnp.concatenate([masks[p] for p in pieces], axis=0)
        carried = attend(queries, arrived, mask, carried, last)
    return carried[None]


def solution(mesh):
    return jax.shard_map(
        per_device,
        mesh=mesh,
        in_specs=(
            P("section", "ctx", "tp"),
            P("section", "ctx", "tp"),
            P("section", "ctx", "tp"),
            P("section", None),
        ),
        out_specs=P("section", "ctx", "tp"),
        check_vma=False,
    )
```

```python
from functools import partial
import math

import jax
import jax.numpy as jnp
import numpy as np
from jax import lax
from jax.experimental import pallas as pl
from jax.experimental.pallas import tpu as pltpu
from jax.sharding import PartitionSpec as P

HEAD_DIM = 128
MASKED = -1e30
SCALE = math.log2(math.e) / math.sqrt(HEAD_DIM)
HEADS_PER_PASS = 4
GROUPS = ((0, 1, 2), (3,))


def shifted(block, axis, distance):
    devices = range(lax.axis_size(axis))
    route = [((i - distance) % len(devices), i) for i in devices]
    return lax.ppermute(block, axis, route)


def rope_tables():
    index_ids = np.arange(HEAD_DIM // 2) * 1.0
    natural = 500000.0 ** (-2.0 * index_ids / HEAD_DIM)
    wavelength = 2.0 * math.pi / natural
    smooth = (8192.0 / wavelength - 1.0) / 3.0
    blended = (1.0 - smooth) * natural / 8.0 + smooth * natural
    scaled = np.where(
        wavelength < 2048.0, natural, np.where(wavelength > 8192.0, natural / 8.0, blended)
    )
    coarse = np.mod(1024.0 * scaled, 2.0 * math.pi)
    sign = np.repeat(np.array([-1.0, 1.0]), HEAD_DIM // 2)
    return [jnp.asarray(table, jnp.float32) for table in (np.tile(scaled, 2), np.tile(coarse, 2), sign)]


def turn_tables(token_pos):
    fine, coarse, sign = rope_tables()
    upper_part = (token_pos // 1024).astype(jnp.float32)
    lower_part = (token_pos % 1024).astype(jnp.float32)
    angles = upper_part[:, None] * coarse[None, :] + lower_part[:, None] * fine[None, :]
    return jnp.cos(angles), jnp.sin(angles) * sign[None, :]


def turned(head, cosine, sine):
    head = head.astype(jnp.float32)
    return (head * cosine + pltpu.roll(head, HEAD_DIM // 2, 1) * sine).astype(jnp.bfloat16)


def turned_rows(rows, cosine, sine):
    half = rows.shape[1] // 2
    heads = [turned(rows[:, i : i + HEAD_DIM], cosine, sine) for i in range(0, half, HEAD_DIM)]
    return jnp.concatenate(heads + [rows[:, half:]], axis=1)


def turn_pair_kernel(own_ref, partner_ref, cosine_ref, sine_ref, out_ref):
    count = own_ref.shape[0]
    for i, ref in enumerate((own_ref, partner_ref)):
        place = pl.ds(i * count, count)
        out_ref[place] = turned_rows(ref[...], cosine_ref[place], sine_ref[place])


WHOLE = pl.BlockSpec(memory_space=pltpu.VMEM)
SMALL = pltpu.CompilerParams(vmem_limit_bytes=8 * 1024 * 1024)


def turn_pair(own_rows, partner_rows, cosine, sine):
    rows, width = own_rows.shape
    return pl.pallas_call(
        turn_pair_kernel,
        in_specs=[WHOLE] * 4,
        out_specs=WHOLE,
        out_shape=jax.ShapeDtypeStruct((2 * rows, width), jnp.bfloat16),
        compiler_params=SMALL,
        name="turn_pair",
    )(own_rows, partner_rows, cosine, sine)


def turn_kernel(query_ref, cosine_ref, sine_ref, out_ref):
    rows = query_ref.shape[0]
    cosine, sine = cosine_ref[:rows], sine_ref[:rows]
    for head in range(query_ref.shape[1] // HEAD_DIM):
        out_ref[head * rows : (head + 1) * rows, :] = turned(
            query_ref[:, head * HEAD_DIM : (head + 1) * HEAD_DIM], cosine, sine
        )


def turn_queries(query_in, cosine, sine):
    rows, width = query_in.shape
    heads = width // HEAD_DIM
    return pl.pallas_call(
        turn_kernel,
        in_specs=[WHOLE] * 3,
        out_specs=WHOLE,
        out_shape=jax.ShapeDtypeStruct((heads * rows, HEAD_DIM), jnp.bfloat16),
        compiler_params=pltpu.CompilerParams(vmem_limit_bytes=8 * 1024 * 1024),
        name="turn",
    )(query_in, cosine, sine)


def attend_kernel(*refs, pieces, first, last):
    refs = list(refs)
    query_ref, *piece_refs = refs[: 1 + pieces]
    mask_ref = refs[1 + pieces]
    refs = refs[2 + pieces :]
    if not first:
        before_ref, before_highest_ref = refs[:2]
        refs = refs[2:]
    if last:
        out_ref, held_ref, sent = refs
    else:
        sums_ref, highest_ref = refs
    tokens, rows = mask_ref.shape
    key_heads = piece_refs[0].shape[1] // (2 * HEAD_DIM)
    size = HEADS_PER_PASS * rows
    steps = query_ref.shape[0] // key_heads // size
    own = lax.broadcasted_iota(jnp.int32, (size, rows), 0) % rows
    one_hot = (own == lax.broadcasted_iota(jnp.int32, (size, rows), 1)).astype(jnp.bfloat16)
    mask = mask_ref[...]
    ones = jnp.ones((tokens, HEAD_DIM), jnp.bfloat16)

    def part(index):
        columns = pl.ds(index * HEAD_DIM, HEAD_DIM)
        return jnp.concatenate([ref[:, columns] for ref in piece_refs], axis=0)

    def score(keys, step):
        queries = jnp.concatenate([query_ref[step * size : (step + 1) * size, :], one_hot], axis=1)
        return lax.dot_general(
            queries, keys, (((1,), (1,)), ((), ())), preferred_element_type=jnp.float32
        )

    copies = []
    keys = [jnp.concatenate([part(i), mask], axis=1) for i in range(key_heads)]
    following = score(keys[0], 0)
    for key_head in range(key_heads):
        values = jnp.concatenate([part(key_heads + key_head), ones], axis=1)
        for step in range(key_head * steps, (key_head + 1) * steps):
            place = pl.ds(step * size, size)
            scores = following
            if step + 1 < key_heads * steps:
                following = score(keys[(step + 1) // steps], step + 1)
            highest = jnp.broadcast_to(jnp.max(scores, axis=-1, keepdims=True), (size, HEAD_DIM))
            if not first:
                before = before_highest_ref[place]
                highest = jnp.maximum(highest, before)
            weights = jnp.concatenate(
                [
                    jnp.exp2((scores[:, i : i + HEAD_DIM] - highest) * SCALE).astype(jnp.bfloat16)
                    for i in range(0, tokens, HEAD_DIM)
                ],
                axis=1,
            )
            summed = lax.dot_general(
                weights, values, (((1,), (0,)), ((), ())), preferred_element_type=jnp.float32
            )
            if not first:
                factor = jnp.exp2((before - highest) * SCALE)
                summed = summed + before_ref[place] * jnp.concatenate([factor, factor], axis=1)
            if not last:
                sums_ref[place] = summed
                highest_ref[place] = highest
                continue
            attended = (summed[:, :HEAD_DIM] / summed[:, HEAD_DIM:]).astype(jnp.bfloat16)
            first_column = step * HEADS_PER_PASS * HEAD_DIM
            held_ref[:, first_column : first_column + HEADS_PER_PASS * HEAD_DIM] = jnp.concatenate(
                [attended[i * rows : (i + 1) * rows] for i in range(HEADS_PER_PASS)], axis=1
            )
            columns = pl.ds(step * HEADS_PER_PASS * HEAD_DIM, HEADS_PER_PASS * HEAD_DIM)
            copies.append(
                pltpu.make_async_copy(held_ref.at[:, columns], out_ref.at[:, columns], sent.at[step])
            )
            copies[-1].start()
    for copy in copies:
        copy.wait()


def attend(queries, pieces, mask, carried, last):
    tokens, rows = mask.shape
    count = queries.shape[0]
    heads = count // rows
    if last:
        out_specs = pl.BlockSpec(memory_space=pl.ANY)
        out_shape = jax.ShapeDtypeStruct((rows, heads * HEAD_DIM), jnp.bfloat16)
        scratch = [
            pltpu.VMEM((rows, heads * HEAD_DIM), jnp.bfloat16),
            pltpu.SemaphoreType.DMA((heads // HEADS_PER_PASS,)),
        ]
    else:
        out_specs = [WHOLE] * 2
        out_shape = [
            jax.ShapeDtypeStruct((count, 2 * HEAD_DIM), jnp.float32),
            jax.ShapeDtypeStruct((count, HEAD_DIM), jnp.float32),
        ]
        scratch = []
    operands = [queries, *pieces, mask, *carried]
    return pl.pallas_call(
        partial(attend_kernel, pieces=len(pieces), first=not carried, last=last),
        in_specs=[WHOLE] * len(operands),
        out_specs=out_specs,
        out_shape=out_shape,
        scratch_shapes=scratch,
        compiler_params=pltpu.CompilerParams(vmem_limit_bytes=24 * 1024 * 1024),
        cost_estimate=pl.CostEstimate(flops=1000, bytes_accessed=1000, transcendentals=0),
        name="attend",
    )(*operands)


def per_device(query_rows, key_rows, value_rows, positions):
    local_rows = query_rows.shape[1]
    sections, owners = lax.axis_size("section"), lax.axis_size("ctx")
    rows = jnp.concatenate([key_rows[0], value_rows[0]], axis=1)
    own_rows = shifted(rows, "section", 1)
    partner_rows = lax.ppermute(
        rows,
        ("section", "ctx"),
        [
            ((s - 1) % sections * owners + (c ^ 1), s * owners + c)
            for s in range(sections)
            for c in range(owners)
        ],
    )
    owner_index = lax.axis_index("ctx")
    blocks = positions[0].reshape(owners, local_rows)

    def pair_pos(index):
        return [lax.dynamic_index_in_dim(blocks, i, keepdims=False) for i in (index, index ^ 1)]

    def beside(index, hop):
        return (index + (1 - index % 2 * 2) * hop) % owners

    def route(hop):
        return [(beside(c, hop), c) for c in range(owners)]

    key_pos = [pair_pos(beside(owner_index, hop)) for hop in (0, 2, -1, -3)]
    own_pos = key_pos[0][0]
    cosine, sine = turn_tables(jnp.concatenate(key_pos[0]))
    masks = [
        jnp.where(jnp.concatenate(pos)[:, None] <= own_pos[None, :], 0.0, MASKED).astype(jnp.bfloat16)
        for pos in key_pos
    ]
    query_rows, own_rows = lax.optimization_barrier((query_rows, own_rows))
    query_in = shifted(query_rows, "section", 1)
    pair_rows = turn_pair(own_rows, partner_rows, cosine, sine)
    second = lax.ppermute(pair_rows, "ctx", route(2))
    beside_rows = lax.ppermute(pair_rows, "ctx", route(-1))
    second, masks = lax.optimization_barrier((second, masks))
    across = lax.ppermute(second, "ctx", route(-1))
    queries = turn_queries(query_in[0], cosine, sine)
    carried = ()
    for i, pieces in enumerate(GROUPS):
        last = i + 1 == len(GROUPS)
        arrived = [(pair_rows, second, beside_rows, across)[p] for p in pieces]
        mask = jnp.concatenate([masks[p] for p in pieces], axis=0)
        carried = attend(queries, arrived, mask, carried, last)
    return carried[None]


def solution(mesh):
    return jax.shard_map(
        per_device,
        mesh=mesh,
        in_specs=(
            P("section", "ctx", "tp"),
            P("section", "ctx", "tp"),
            P("section", "ctx", "tp"),
            P("section", None),
        ),
        out_specs=P("section", "ctx", "tp"),
        check_vma=False,
    )
```
